256 devices in a mesh: ctx: 32 (over y, z_hi, x), tp: 8 (over z_lo, core).
Axes of the slice: x: 4, y: 4, z: 8 (z_hi: 2, z_lo: 4; z = z_hi * 4 + z_lo), core: 2. Of those that a mesh axis runs over, the one named last changes fastest.
Arguments:
- query_raw: bfloat16 [4096, 8192], P('ctx', 'tp'), may hold values from -6 to 6
- key_raw: bfloat16 [4096, 1024], P(('ctx', 'tp')), may hold values from -6 to 6
- values: bfloat16 [4096, 1024], P(('ctx', 'tp')), may hold values from -6 to 6
- grad_out: bfloat16 [4096, 8192], P('ctx', 'tp'), may hold values from -96 to 96
Outputs:
- grad_query: bfloat16 [4096, 8192], P('ctx', 'tp')
- grad_key: bfloat16 [4096, 1024], P(('ctx', 'tp'))
- grad_value: bfloat16 [4096, 1024], P(('ctx', 'tp'))
The draws below stay inside these ranges and needn't reach their ends.
All inputs are finite; a program needn't handle non-finite values.
Results may differ from the reference program's by a relative error of at most 0.03.
Values may be sent and summed in bfloat16 or wider, within the bound.
A program may use at most 64 MiB of HBM per device.

```python
import math
import jax
import jax.numpy as jnp
from jax import lax

HEADS = 64
KV_HEADS = 8
HEAD_DIM = 128
TEXT_TOKENS = 4096
IMAGES = 4096


def steps_of(key, shape, shards, least, largest):
    def one(axis_at, parts):
        draws = jax.random.uniform(jax.random.fold_in(jax.random.fold_in(key, 6), axis_at), (parts,), jnp.float32, least / len(shards), largest / len(shards))
        return jnp.repeat(jnp.exp(draws), shape[axis_at] // parts).reshape((-1,) + (1,) * (len(shape) - axis_at - 1))

    level = one(*shards[0])
    for cut in shards[1:]:
        level = level * one(*cut)
    return level


def normal_values(key, shape, width, limit, shards=(), held_as=jnp.bfloat16):
    entries = width * jax.random.normal(key, shape, jnp.float32)
    if shards:
        entries = entries * steps_of(key, shape, shards, -0.22, 0.18)
    return jnp.clip(entries, -limit, limit).astype(held_as)


def setup_inputs(seed: int = 0) -> dict:
    splits = jax.random.split(jax.random.key(seed), 5)
    query_raw = normal_values(splits[0], (TEXT_TOKENS, HEADS * HEAD_DIM), 1.0, 6.0, ((0, 32), (1, 8)))
    key_raw = normal_values(splits[1], (IMAGES, KV_HEADS * HEAD_DIM), 1.0, 6.0, ((0, 256),))
    values = normal_values(splits[2], (IMAGES, KV_HEADS * HEAD_DIM), 1.0, 6.0, ((0, 256),))
    grad_out = normal_values(splits[3], (TEXT_TOKENS, HEADS * HEAD_DIM), 16.0, 96.0, ((0, 32), (1, 8)))
    return dict(query_raw=query_raw, key_raw=key_raw, values=values, grad_out=grad_out)


epsilon = 1e-06

def unit_rows(raw_values):
    widened = raw_values.astype(jnp.float32)
    factor = lax.rsqrt(lax.optimization_barrier(jnp.mean(widened * widened, axis=-1, keepdims=True)) + epsilon)
    return (widened * factor, factor)

def unit_back(upstream_grad, unit_values, factor):
    return factor * (upstream_grad - unit_values * lax.optimization_barrier(jnp.mean(upstream_grad * unit_values, axis=-1, keepdims=True)))

def head_grad(queries, upstream, key_rows, value_rows):
    row_count = queries.shape[0]
    key_count = key_rows.shape[0]
    inv_root = 1.0 / math.sqrt(key_rows.shape[1])
    block_len = math.gcd(key_count, 512)
    block_count = key_count // block_len
    key_blocks = key_rows.reshape(block_count, block_len, key_rows.shape[1])
    value_blocks = value_rows.reshape(block_count, block_len, value_rows.shape[1])

    def accumulate(running, pieces):
        key_block, value_block = pieces
        raised = jnp.exp(jnp.dot(queries, key_block.T, preferred_element_type=jnp.float32) * inv_root)
        value_dots = jnp.dot(upstream, value_block.T, preferred_element_type=jnp.float32)
        return ((running[0] + lax.optimization_barrier(jnp.sum(raised, axis=1)), running[1] + lax.optimization_barrier(jnp.sum(raised * value_dots, axis=1))), None)
    start = jnp.zeros((row_count,), jnp.float32)
    (totals, weighted), unused = lax.scan(accumulate, (start, start), (key_blocks, value_blocks))
    delta_row = weighted / totals

    def backward_block(query_acc, pieces):
        key_block, value_block = pieces
        raised = jnp.exp(jnp.dot(queries, key_block.T, preferred_element_type=jnp.float32) * inv_root)
        attend = raised / totals[:, None]
        attend_cast = attend.astype(jnp.bfloat16)
        value_dots = jnp.dot(upstream, value_block.T, preferred_element_type=jnp.float32)
        score_grad = (attend * (value_dots - delta_row[:, None])).astype(jnp.bfloat16)
        query_acc = query_acc + jnp.dot(score_grad, key_block, preferred_element_type=jnp.float32) * inv_root
        key_piece = jnp.dot(score_grad.T, queries, preferred_element_type=jnp.float32) * inv_root
        value_piece = jnp.dot(attend_cast.T, upstream, preferred_element_type=jnp.float32)
        return (query_acc, (key_piece, value_piece))
    query_grad, (key_grad, value_grad) = lax.scan(backward_block, jnp.zeros((row_count, queries.shape[1]), jnp.float32), (key_blocks, value_blocks))
    return (query_grad, key_grad.reshape(key_count, -1), value_grad.reshape(key_count, -1))

def reference(query_raw, key_raw, values, grad_out):
    text_rows = query_raw.shape[0]
    group_size = HEADS // KV_HEADS
    query_unit, query_scale = unit_rows(query_raw.reshape(text_rows, KV_HEADS, group_size, HEAD_DIM))
    key_unit, key_scale = unit_rows(key_raw.reshape(IMAGES, KV_HEADS, HEAD_DIM))
    queries = query_unit.astype(jnp.bfloat16).transpose(1, 0, 2, 3).reshape(KV_HEADS, text_rows * group_size, HEAD_DIM)
    upstream = grad_out.reshape(text_rows, KV_HEADS, group_size, HEAD_DIM).transpose(1, 0, 2, 3).reshape(KV_HEADS, text_rows * group_size, HEAD_DIM)
    key_heads = key_unit.astype(jnp.bfloat16).transpose(1, 0, 2)
    value_heads = values.reshape(IMAGES, KV_HEADS, HEAD_DIM).transpose(1, 0, 2)
    query_grad, key_grad, value_grad = lax.map(lambda bundle: head_grad(bundle[0], bundle[1], bundle[2], bundle[3]), (queries, upstream, key_heads, value_heads))
    query_grad = query_grad.reshape(KV_HEADS, text_rows, group_size, HEAD_DIM).transpose(1, 0, 2, 3)
    grad_query = unit_back(query_grad, query_unit, query_scale).astype(jnp.bfloat16).reshape(text_rows, HEADS * HEAD_DIM)
    key_grad = key_grad.transpose(1, 0, 2)
    grad_key = unit_back(key_grad, key_unit, key_scale).astype(jnp.bfloat16).reshape(IMAGES, KV_HEADS * HEAD_DIM)
    grad_value = value_grad.transpose(1, 0, 2).reshape(IMAGES, KV_HEADS * HEAD_DIM).astype(jnp.bfloat16)
    return (grad_query, grad_key, grad_value)
```

```python
import math

import jax
import jax.numpy as jnp
from jax import lax
from jax.experimental import pallas as pl
from jax.experimental.pallas import tpu as pltpu
from jax.sharding import PartitionSpec as P

F32 = jnp.float32
BF16 = jnp.bfloat16
MESH = pl.DeviceIdType.MESH
EPS = 1e-6
D = 128
HEADS = 8
ROWS = 1024
BLOCK = 256
HALF = BLOCK // 2
LINE = 16
INV = 1.0 / math.sqrt(D)
EXP2 = INV * math.log2(math.e)

ORDER = (
    ((0, 0),),
    ((1, 0), (3, 0), (0, 1), (0, 3)),
    ((1, 1), (1, 3), (3, 1), (3, 3)),
    ((2, 0), (0, 2)),
    ((1, 2), (3, 2), (2, 1), (2, 3)),
    ((2, 2),),
)
PLACE = {at: n for n, at in enumerate(sum(ORDER, ()))}
GROUPS = []
for group in ORDER:
    GROUPS.append((PLACE[group[0]], PLACE[group[-1]] + 1))


def unit(raw):
    scale = lax.rsqrt(jnp.mean(raw * raw, axis=-1, keepdims=True) + EPS)
    return raw * scale, scale


def unit_back(grad, unit_rows, scale):
    return scale * (grad - unit_rows * jnp.mean(grad * unit_rows, axis=-1, keepdims=True))


def place(kind, a, b):
    a, b = a % 4, b % 4
    return PLACE[(a, b) if kind == 0 else (b, a)]


def kernel(
    q_ref, k_ref, v_ref, do_ref,
    gq_ref, gk_ref, gv_ref,
    q_t, do_t, q_n, do_n, raised, dots, totals, weighted, rows, dq_t,
    mine, kv, part, piece_in, full_in, last_piece, last_full, line_in,
    z_send, z_recv, y_send, y_recv, send, recv, r_send, p_recv, f_recv, lp_recv, lf_recv,
):
    ctx = lax.axis_index("ctx")
    tp = lax.axis_index("tp")
    y, z_hi, x = ctx // 8, (ctx // 4) % 2, ctx % 4
    me = z_hi * 8 + tp

    def beside(axis, step):
        if axis == 0:
            return (y * 8 + z_hi * 4 + (x + step) % 4, tp)
        return (((y + step) % 4) * 8 + z_hi * 4 + x, tp)

    def on_line(step):
        other = (me + step) % LINE
        return (y * 8 + (other // 8) * 4 + x, other % 8)

    barrier = pltpu.get_barrier_semaphore()

    def greet(step, carry):
        pl.semaphore_signal(barrier, inc=1, device_id=on_line(step), device_id_type=MESH)
        return carry

    lax.fori_loop(1, LINE, greet, 0)
    for axis in range(2):
        for step in (1, 3):
            pl.semaphore_signal(barrier, inc=1, device_id=beside(axis, step), device_id_type=MESH)

    for h in range(HEADS):
        cols = slice(h * D, (h + 1) * D)
        mine[h, 0] = unit(k_ref[:, cols].astype(F32))[0].astype(BF16)
        mine[h, 1] = v_ref[:, cols]
    pl.semaphore_wait(barrier, LINE - 1 + 4)

    def z_copy(step):
        target = on_line(step)
        spot = pl.multiple_of((LINE - step) * 16, 16)
        return pltpu.make_async_remote_copy(
            src_ref=mine.at[target[1]],
            dst_ref=kv.at[0, :, pl.ds(spot, 16), :],
            send_sem=z_send.at[step],
            recv_sem=z_recv.at[step],
            device_id=target,
            device_id_type=MESH,
        )

    def z_start(step, carry):
        z_copy(step).start()
        return carry

    lax.fori_loop(1, LINE, z_start, 0)
    kv[0, :, 0:16, :] = mine[tp]

    for h in range(HEADS):
        cols = slice(h * D, (h + 1) * D)
        cast = unit(q_ref[:, cols].astype(F32))[0].astype(BF16)
        q_n[cols, :] = cast
        q_t[:, cols] = cast.T
        do_n[cols, :] = do_ref[:, cols]
        do_t[:, cols] = do_ref[:, cols].T
    totals[...] = jnp.zeros_like(totals)
    weighted[...] = jnp.zeros_like(weighted)
    dq_t[...] = jnp.zeros_like(dq_t)

    def z_wait(step, carry):
        copy = z_copy(step)
        copy.wait_send()
        copy.wait_recv()
        return carry

    lax.fori_loop(1, LINE, z_wait, 0)

    def pass_1(n, carry):
        scores = jnp.dot(kv[n, 0], q_t[...], preferred_element_type=F32)
        value_dots = jnp.dot(kv[n, 1], do_t[...], preferred_element_type=F32)
        e = jnp.exp2(scores * EXP2)
        raised[n] = e
        dots[n] = value_dots
        totals[...] += jnp.sum(e.reshape(BLOCK // 8, 8, ROWS), axis=0)
        weighted[...] += jnp.sum((e * value_dots).reshape(BLOCK // 8, 8, ROWS), axis=0)
        return carry

    started = []

    def rows_of(half):
        return slice(0, BLOCK) if half is None else slice(half * HALF, (half + 1) * HALF)

    def gather_copy(kind, a, b, axis_of, step, half):
        src = place(kind, a, b)
        dst = place(kind, a - step, b) if axis_of == 0 else place(kind, a, b - step)
        axis = axis_of if kind == 0 else 1 - axis_of
        return pltpu.make_async_remote_copy(
            src_ref=kv.at[src, kind, rows_of(half), :],
            dst_ref=kv.at[dst, kind, rows_of(half), :],
            send_sem=send.at[len(started)],
            recv_sem=recv.at[dst, kind, half or 0],
            device_id=beside(axis, step % 4),
            device_id_type=MESH,
        )

    def forward(a, b, axis_of, step, half=None):
        for kind in range(2):
            copy = gather_copy(kind, a, b, axis_of, step, half)
            copy.start()
            started.append(copy)

    def arrived(a, b, half=None):
        for kind in range(2):
            at = place(kind, a, b)
            ref = kv.at[at, kind, rows_of(half), :]
            pltpu.make_async_copy(ref, ref, recv.at[at, kind, half or 0]).wait()

    def run(body, group):
        lax.fori_loop(*GROUPS[group], body, 0)

    for axis_of in range(2):
        for step in (1, -1):
            forward(0, 0, axis_of, step)
    run(pass_1, 0)
    for a in (1, 3):
        arrived(a, 0)
        forward(a, 0, 0, a - 2, half=1 if a == 1 else 0)
    for a in (1, 3):
        for step in (1, -1):
            forward(a, 0, 1, step)
    arrived(0, 1)
    forward(0, 1, 1, -1, half=1)
    arrived(0, 3)
    forward(0, 3, 1, 1, half=0)
    run(pass_1, 1)
    arrived(2, 0, 0)
    arrived(2, 0, 1)
    for step in (1, -1):
        forward(2, 0, 1, step)
    for a in (1, 3):
        arrived(a, 1)
        forward(a, 1, 1, -1, half=1)
        arrived(a, 3)
        forward(a, 3, 1, 1, half=0)
    run(pass_1, 2)
    arrived(0, 2, 0)
    arrived(0, 2, 1)
    arrived(2, 1)
    forward(2, 1, 1, -1, half=1)
    arrived(2, 3)
    forward(2, 3, 1, 1, half=0)
    run(pass_1, 3)
    for a in (1, 3):
        arrived(a, 2, 0)
        arrived(a, 2, 1)
    run(pass_1, 4)
    arrived(2, 2, 0)
    arrived(2, 2, 1)
    run(pass_1, 5)
    for copy in started:
        copy.wait_send()

    total = jnp.sum(totals[...], axis=0, keepdims=True)
    inverse = 1.0 / total
    rows[0:1, :] = inverse
    rows[1:2, :] = jnp.sum(weighted[...], axis=0, keepdims=True) * inverse

    def pass_2(n, carry):
        attend = raised[n] * rows[0:1, :]
        score_grad = (attend * (dots[n] - rows[1:2, :])).astype(BF16)
        part[n, 1] = jnp.dot(attend.astype(BF16), do_n[...], preferred_element_type=F32).astype(BF16)
        part[n, 0] = (jnp.dot(score_grad, q_n[...], preferred_element_type=F32) * INV).astype(BF16)
        dq_t[...] += jnp.dot(kv[n, 0].T, score_grad, preferred_element_type=F32)
        return carry

    sent = []

    def give(kind, src, dst, sem, axis, step):
        copy = pltpu.make_async_remote_copy(
            src_ref=src,
            dst_ref=dst,
            send_sem=r_send.at[len(sent)],
            recv_sem=sem,
            device_id=beside(axis, step % 4),
            device_id_type=MESH,
        )
        copy.start()
        sent.append(copy)

    def take(ref, sem):
        pltpu.make_async_copy(ref, ref, sem).wait()

    def add(at, kind, half, *refs):
        where = (at, kind, rows_of(half), slice(None))
        value = part[where].astype(F32)
        for ref in refs:
            value = value + ref[...].astype(F32)
        part[where] = value.astype(BF16)

    def far(a, b, axis_of, pieces, sems, index):
        for kind in range(2):
            axis = axis_of if kind == 0 else 1 - axis_of
            at = place(kind, a, b)
            for half, step in ((0, 1), (1, -1)):
                give(kind, part.at[at, kind, rows_of(half), :], pieces.at[(kind, *index, half)],
                     sems.at[(kind, *index, half)], axis, step)

    def near(a, b, axis_of, step, pieces, p_sems, fulls, f_sems, index):
        half = 0 if step == 1 else 1
        for kind in range(2):
            axis = axis_of if kind == 0 else 1 - axis_of
            at = place(kind, a, b)
            take(pieces.at[(kind, *index, half)], p_sems.at[(kind, *index, half)])
            add(at, kind, half, pieces.at[(kind, *index, half)])
            give(kind, part.at[at, kind], fulls.at[(kind, *index, half)], f_sems.at[(kind, *index, half)], axis, step)

    def own(a, b, fulls, f_sems, index):
        for kind in range(2):
            at = place(kind, a, b)
            for side in range(2):
                take(fulls.at[(kind, *index, side)], f_sems.at[(kind, *index, side)])
            add(at, kind, None, fulls.at[(kind, *index, 0)], fulls.at[(kind, *index, 1)])

    def far_1(a):
        far(a, 2, 1, piece_in, p_recv, (a,))

    def near_1(a, b):
        near(a, b, 1, 1 if b == 1 else -1, piece_in, p_recv, full_in, f_recv, (a,))

    def own_1(a):
        own(a, 0, full_in, f_recv, (a,))

    run(pass_2, 5)
    far_1(2)
    run(pass_2, 4)
    far_1(1)
    far_1(3)
    near_1(2, 1)
    near_1(2, 3)
    run(pass_2, 3)
    far_1(0)
    run(pass_2, 2)
    for a in (1, 3):
        for b in (1, 3):
            near_1(a, b)
    own_1(2)
    far(2, 0, 0, last_piece, lp_recv, ())
    run(pass_2, 1)
    near_1(0, 1)
    near_1(0, 3)
    run(pass_2, 0)
    for a in (1, 3):
        own_1(a)
        near(a, 0, 0, 1 if a == 1 else -1, last_piece, lp_recv, last_full, lf_recv, ())

    for h in range(HEADS):
        cols = slice(h * D, (h + 1) * D)
        unit_rows, scale = unit(q_ref[:, cols].astype(F32))
        gq_ref[:, cols] = unit_back(dq_t[:, cols].T * INV, unit_rows, scale).astype(BF16)

    own_1(0)
    own(0, 0, last_full, lf_recv, ())

    def line_copy(step):
        spot = pl.multiple_of(step * 16, 16)
        return pltpu.make_async_remote_copy(
            src_ref=part.at[0, :, pl.ds(spot, 16), :],
            dst_ref=line_in.at[me],
            send_sem=y_send.at[step],
            recv_sem=y_recv.at[step],
            device_id=on_line(step),
            device_id_type=MESH,
        )

    def line_start(step, carry):
        line_copy(step).start()
        return carry

    lax.fori_loop(1, LINE, line_start, 0)
    line_in[me] = part[0, :, 0:16, :]
    for copy in sent:
        copy.wait_send()

    def line_wait(step, carry):
        copy = line_copy(step)
        copy.wait_send()
        came = line_in.at[(me + LINE - step) % LINE]
        pltpu.make_async_copy(came, came, y_recv.at[step]).wait()
        return carry

    lax.fori_loop(1, LINE, line_wait, 0)
    for h in range(HEADS):
        cols = slice(h * D, (h + 1) * D)
        sums = line_in[h].astype(F32) + line_in[h + 8].astype(F32)
        unit_rows, scale = unit(k_ref[:, cols].astype(F32))
        gk_ref[:, cols] = unit_back(sums[0], unit_rows, scale).astype(BF16)
        gv_ref[:, cols] = sums[1].astype(BF16)


def shards(query_raw, key_raw, values, grad_out):
    vmem = pl.BlockSpec(memory_space=pltpu.VMEM)
    dma = pltpu.SemaphoreType.DMA
    return pl.pallas_call(
        kernel,
        out_shape=[
            jax.ShapeDtypeStruct(query_raw.shape, BF16),
            jax.ShapeDtypeStruct(key_raw.shape, BF16),
            jax.ShapeDtypeStruct(values.shape, BF16),
        ],
        in_specs=[vmem] * 4,
        out_specs=[vmem] * 3,
        scratch_shapes=[
            pltpu.VMEM((D, ROWS), BF16),
            pltpu.VMEM((D, ROWS), BF16),
            pltpu.VMEM((ROWS, D), BF16),
            pltpu.VMEM((ROWS, D), BF16),
            pltpu.VMEM((16, BLOCK, ROWS), F32),
            pltpu.VMEM((16, BLOCK, ROWS), F32),
            pltpu.VMEM((8, ROWS), F32),
            pltpu.VMEM((8, ROWS), F32),
            pltpu.VMEM((8, ROWS), F32),
            pltpu.VMEM((D, ROWS), F32),
            pltpu.VMEM((HEADS, 2, 16, D), BF16),
            pltpu.VMEM((16, 2, BLOCK, D), BF16),
            pltpu.VMEM((16, 2, BLOCK, D), BF16),
            pltpu.VMEM((2, 4, 2, HALF, D), BF16),
            pltpu.VMEM((2, 4, 2, BLOCK, D), BF16),
            pltpu.VMEM((2, 2, HALF, D), BF16),
            pltpu.VMEM((2, 2, BLOCK, D), BF16),
            pltpu.VMEM((LINE, 2, 16, D), BF16),
            dma((LINE,)),
            dma((LINE,)),
            dma((LINE,)),
            dma((LINE,)),
            dma((40,)),
            dma((16, 2, 2)),
            dma((40,)),
            dma((2, 4, 2)),
            dma((2, 4, 2)),
            dma((2, 2)),
            dma((2, 2)),
        ],
        compiler_params=pltpu.CompilerParams(
            collective_id=0, has_side_effects=True, vmem_limit_bytes=56 * 2**20
        ),
    )(query_raw, key_raw, values, grad_out)


def solution(mesh):
    split = (P("ctx", "tp"), P(("ctx", "tp"), None), P(("ctx", "tp"), None), P("ctx", "tp"))
    return jax.shard_map(
        shards, mesh=mesh, in_specs=split, out_specs=split[:3], check_vma=False
    )
```

```python
import math

import jax
import jax.numpy as jnp
from jax import lax
from jax.experimental import pallas as pl
from jax.experimental.pallas import tpu as pltpu
from jax.sharding import PartitionSpec as P

F32 = jnp.float32
BF16 = jnp.bfloat16
MESH = pl.DeviceIdType.MESH
EPS = 1e-6
D = 128
HEADS = 8
ROWS = 1024
BLOCK = 256
HALF = BLOCK // 2
LINE = 16
INV = 1.0 / math.sqrt(D)
EXP2 = INV * math.log2(math.e)
KEYS, VALUES = 0, 1

ORDER = (
    ((0, 0),),
    ((1, 0), (3, 0), (0, 1), (0, 3)),
    ((1, 1), (1, 3), (3, 1), (3, 3)),
    ((2, 0), (0, 2)),
    ((1, 2), (3, 2), (2, 1), (2, 3)),
    ((2, 2),),
)
PLACE = {at: n for n, at in enumerate(sum(ORDER, ()))}
GROUPS = [(PLACE[group[0]], PLACE[group[-1]] + 1) for group in ORDER]
FAR_FIRST = (8, 7, 9, 6, 10, 5, 11, 4, 12, 3, 13, 2, 14, 15, 1)

G_FIRST = 1
G_SECOND = 4
R_FIRST = 1
R_SECOND = 0


def unit(raw):
    scale = lax.rsqrt(jnp.mean(raw * raw, axis=-1, keepdims=True) + EPS)
    return raw * scale, scale


def unit_back(grad, unit_rows, scale):
    return scale * (grad - unit_rows * jnp.mean(grad * unit_rows, axis=-1, keepdims=True))


def place(kind, a, b):
    a, b = a % 4, b % 4
    return PLACE[(a, b) if kind == KEYS else (b, a)]


def rows_of(half):
    return slice(0, BLOCK) if half is None else slice(half * HALF, (half + 1) * HALF)


def kernel(
    q_in, k_ref, v_ref, do_in,
    gq_ref, gk_ref, gv_ref,
    q_ref, do_ref, q_t, do_t, q_n, do_n, raised, dots, totals, weighted, rows, dq_t,
    mine, kv, part, piece_in, full_in, last_piece, last_full, line_in,
    load, z_sem, y_sem, send, recv, r_send, p_recv, f_recv, l_recv,
):
    ctx = lax.axis_index("ctx")
    tp = lax.axis_index("tp")
    y, z_hi, x = ctx // 8, (ctx // 4) % 2, ctx % 4
    me = z_hi * 8 + tp

    def beside(kind, axis, step):
        if axis == kind:
            return (y * 8 + z_hi * 4 + (x + step) % 4, tp)
        return (((y + step) % 4) * 8 + z_hi * 4 + x, tp)

    def on_line(step):
        other = (me + step) % LINE
        return (y * 8 + (other // 8) * 4 + x, other % 8)

    def take(ref, sem):
        pltpu.make_async_copy(ref, ref, sem).wait()

    q_load = pltpu.make_async_copy(q_in, q_ref, load.at[0])
    do_load = pltpu.make_async_copy(do_in, do_ref, load.at[1])
    q_load.start()
    do_load.start()
    barrier = pltpu.get_barrier_semaphore()
    for step in FAR_FIRST:
        pl.semaphore_signal(barrier, inc=1, device_id=on_line(step), device_id_type=MESH)
    for axis in range(2):
        for step in (1, 2, 3):
            pl.semaphore_signal(barrier, inc=1, device_id=beside(KEYS, axis, step), device_id_type=MESH)

    for h in range(HEADS):
        cols = slice(h * D, (h + 1) * D)
        mine[h, KEYS] = unit(k_ref[:, cols].astype(F32))[0].astype(BF16)
        mine[h, VALUES] = v_ref[:, cols]
    totals[...] = jnp.zeros_like(totals)
    weighted[...] = jnp.zeros_like(weighted)
    dq_t[...] = jnp.zeros_like(dq_t)
    pl.semaphore_wait(barrier, LINE - 1 + 6)

    for step in FAR_FIRST:
        target = on_line(step)
        pltpu.make_async_remote_copy(
            src_ref=mine.at[target[1]],
            dst_ref=kv.at[0, :, pl.ds((LINE - step) * 16, 16), :],
            send_sem=z_sem.at[0],
            recv_sem=z_sem.at[1],
            device_id=target,
            device_id_type=MESH,
        ).start()
    kv[0, :, 0:16, :] = mine[tp]

    q_load.wait()
    do_load.wait()
    for h in range(HEADS):
        cols = slice(h * D, (h + 1) * D)
        cast = unit(q_ref[:, cols].astype(F32))[0].astype(BF16)
        q_n[cols, :] = cast
        q_t[:, cols] = cast.T
        do_n[cols, :] = do_ref[:, cols]
        do_t[:, cols] = do_ref[:, cols].T

    others = kv.at[0, :, 16:BLOCK, :]
    take(others, z_sem.at[1])

    def forward(a, b, axis, step, half=None):
        for kind in range(2):
            src = place(kind, a, b)
            to = ((a - step) % 4, b) if axis == 0 else (a, (b - step) % 4)
            pltpu.make_async_remote_copy(
                src_ref=kv.at[src, kind, rows_of(half), :],
                dst_ref=kv.at[place(kind, *to), kind, rows_of(half), :],
                send_sem=send,
                recv_sem=recv.at[to],
                device_id=beside(kind, axis, step % 4),
                device_id_type=MESH,
            ).start()

    def straight(a):
        return G_SECOND >> a & 1

    def out_second(a):
        for step in (1, -1) + ((2,) if straight(a) else ()):
            forward(a, 0, 1, step)

    def got(a, b):
        take(kv.at[0], recv.at[a, b])
        if b in (1, 3) and not straight(a):
            forward(a, b, 1, b - 2, half=1 if b == 1 else 0)
        if b == 0 and a in (1, 3) and not G_FIRST:
            forward(a, 0, 0, a - 2, half=1 if a == 1 else 0)

    def run(body, group):
        lax.fori_loop(*GROUPS[group], body, 0)

    def pass_1(n, carry):
        scores = jnp.dot(kv[n, KEYS], q_t[...], preferred_element_type=F32)
        value_dots = jnp.dot(kv[n, VALUES], do_t[...], preferred_element_type=F32)
        e = jnp.exp2(scores * EXP2)
        raised[n] = e
        dots[n] = value_dots
        totals[...] += jnp.sum(e.reshape(BLOCK // 8, 8, ROWS), axis=0)
        weighted[...] += jnp.sum((e * value_dots).reshape(BLOCK // 8, 8, ROWS), axis=0)
        return carry

    for step in (1, -1) + ((2,) if G_FIRST else ()):
        forward(0, 0, 0, step)
    out_second(0)
    run(pass_1, 0)
    got(1, 0)
    got(3, 0)
    out_second(1)
    out_second(3)
    if G_FIRST:
        got(2, 0)
        out_second(2)
    got(0, 1)
    got(0, 3)
    run(pass_1, 1)
    if not G_FIRST:
        got(2, 0)
        out_second(2)
    for a in (1, 3):
        got(a, 1)
        got(a, 3)
    run(pass_1, 2)
    got(0, 2)
    got(2, 1)
    got(2, 3)
    run(pass_1, 3)
    got(1, 2)
    got(3, 2)
    run(pass_1, 4)
    got(2, 2)
    run(pass_1, 5)

    total = jnp.sum(totals[...], axis=0, keepdims=True)
    inverse = 1.0 / total
    rows[0:1, :] = inverse
    rows[1:2, :] = jnp.sum(weighted[...], axis=0, keepdims=True) * inverse

    def pass_2(n, carry):
        attend = raised[n] * rows[0:1, :]
        score_grad = (attend * (dots[n] - rows[1:2, :])).astype(BF16)
        part[n, VALUES] = jnp.dot(attend.astype(BF16), do_n[...], preferred_element_type=F32).astype(BF16)
        part[n, KEYS] = (jnp.dot(score_grad, q_n[...], preferred_element_type=F32) * INV).astype(BF16)
        dq_t[...] += jnp.dot(kv[n, KEYS].T, score_grad, preferred_element_type=F32)
        return carry

    def give(src, dst, sem, kind, axis, step):
        pltpu.make_async_remote_copy(
            src_ref=src,
            dst_ref=dst,
            send_sem=r_send,
            recv_sem=sem,
            device_id=beside(kind, axis, step % 4),
            device_id_type=MESH,
        ).start()

    def add(kind, at, half, *refs):
        where = (at, kind, rows_of(half), slice(None))
        value = part[where].astype(F32)
        for ref in refs:
            value = value + ref[...].astype(F32)
        part[where] = value.astype(BF16)

    def buffers(a, axis):
        if axis == 1:
            return (piece_in.at[a], p_recv.at[a], full_in.at[a], f_recv.at[a], R_SECOND >> a & 1)
        return (last_piece, l_recv, last_full, l_recv.at[2], R_FIRST)

    def far(a, b, axis):
        pieces, p_sems, fulls, f_sem, direct = buffers(a, axis)
        for kind in range(2):
            at = place(kind, a, b)
            if direct:
                give(part.at[at, kind], fulls.at[kind, 2], f_sem, kind, axis, 2)
                continue
            for half, step in ((0, 1), (1, -1)):
                give(part.at[at, kind, rows_of(half), :], pieces.at[kind, half], p_sems.at[half], kind, axis, step)

    def near(a, b, axis):
        pieces, p_sems, fulls, f_sem, direct = buffers(a, axis)
        step = 2 - (a if axis == 0 else b)
        half = 0 if step == 1 else 1
        if not direct:
            take(kv.at[0, 0], p_sems.at[half])
        for kind in range(2):
            at = place(kind, a, b)
            if not direct:
                add(kind, at, half, pieces.at[kind, half])
            give(part.at[at, kind], fulls.at[kind, half], f_sem, kind, axis, step)

    def own(a, axis):
        pieces, p_sems, fulls, f_sem, direct = buffers(a, axis)
        sides = 3 if direct else 2
        take(kv.at[0:sides], f_sem)
        for kind in range(2):
            add(kind, place(kind, a, 0), None, *[fulls.at[kind, side] for side in range(sides)])

    run(pass_2, 5)
    far(2, 2, 1)
    run(pass_2, 4)
    far(1, 2, 1)
    far(3, 2, 1)
    near(2, 1, 1)
    near(2, 3, 1)
    run(pass_2, 3)
    far(0, 2, 1)
    run(pass_2, 2)
    for a in (1, 3):
        for b in (1, 3):
            near(a, b, 1)
    own(2, 1)
    far(2, 0, 0)
    run(pass_2, 1)
    near(0, 1, 1)
    near(0, 3, 1)
    run(pass_2, 0)
    for a in (1, 3):
        own(a, 1)
        near(a, 0, 0)

    for h in range(HEADS):
        cols = slice(h * D, (h + 1) * D)
        unit_rows, scale = unit(q_ref[:, cols].astype(F32))
        gq_ref[:, cols] = unit_back(dq_t[:, cols].T * INV, unit_rows, scale).astype(BF16)

    own(0, 1)
    own(0, 0)

    for step in FAR_FIRST:
        pltpu.make_async_remote_copy(
            src_ref=part.at[0, :, pl.ds(step * 16, 16), :],
            dst_ref=line_in.at[me],
            send_sem=y_sem.at[0],
            recv_sem=y_sem.at[1],
            device_id=on_line(step),
            device_id_type=MESH,
        ).start()
    line_in[me] = part[0, :, 0:16, :]
    take(others, z_sem.at[0])
    take(kv.at[0:15], send)
    take(part.at[0:15], r_send)
    take(line_in.at[0 : LINE - 1], y_sem.at[1])
    for h in range(HEADS):
        cols = slice(h * D, (h + 1) * D)
        sums = line_in[h].astype(F32) + line_in[h + 8].astype(F32)
        unit_rows, scale = unit(k_ref[:, cols].astype(F32))
        gk_ref[:, cols] = unit_back(sums[KEYS], unit_rows, scale).astype(BF16)
        gv_ref[:, cols] = sums[VALUES].astype(BF16)
    take(line_in.at[0 : LINE - 1], y_sem.at[0])


def hand_over(*refs):
    for source, target in zip(refs[:3], refs[3:]):
        target[...] = source[...]


def shards(query_raw, key_raw, values, grad_out):
    vmem = pl.BlockSpec(memory_space=pltpu.VMEM)
    anywhere = pl.BlockSpec(memory_space=pl.ANY)
    dma = pltpu.SemaphoreType.DMA
    outs = [jax.ShapeDtypeStruct(a.shape, BF16) for a in (query_raw, key_raw, values)]
    grads = pl.pallas_call(
        kernel,
        out_shape=outs,
        in_specs=[anywhere, vmem, vmem, anywhere],
        out_specs=[vmem] * 3,
        scratch_shapes=[
            pltpu.VMEM((D, ROWS), BF16),
            pltpu.VMEM((D, ROWS), BF16),
            pltpu.VMEM((D, ROWS), BF16),
            pltpu.VMEM((D, ROWS), BF16),
            pltpu.VMEM((ROWS, D), BF16),
            pltpu.VMEM((ROWS, D), BF16),
            pltpu.VMEM((16, BLOCK, ROWS), F32),
            pltpu.VMEM((16, BLOCK, ROWS), F32),
            pltpu.VMEM((8, ROWS), F32),
            pltpu.VMEM((8, ROWS), F32),
            pltpu.VMEM((8, ROWS), F32),
            pltpu.VMEM((D, ROWS), F32),
            pltpu.VMEM((HEADS, 2, 16, D), BF16),
            pltpu.VMEM((16, 2, BLOCK, D), BF16),
            pltpu.VMEM((16, 2, BLOCK, D), BF16),
            pltpu.VMEM((4, 2, 2, HALF, D), BF16),
            pltpu.VMEM((4, 2, 3, BLOCK, D), BF16),
            pltpu.VMEM((2, 2, HALF, D), BF16),
            pltpu.VMEM((2, 3, BLOCK, D), BF16),
            pltpu.VMEM((LINE, 2, 16, D), BF16),
            dma((2,)),
            dma((2,)),
            dma((2,)),
            dma,
            dma((4, 4)),
            dma,
            dma((4, 2)),
            dma((4,)),
            dma((3,)),
        ],
        compiler_params=pltpu.CompilerParams(
            collective_id=0, has_side_effects=True, vmem_limit_bytes=56 * 2**20
        ),
    )(query_raw, key_raw, values, grad_out)
    return pl.pallas_call(hand_over, out_shape=outs, in_specs=[vmem] * 3, out_specs=[vmem] * 3)(*grads)


def solution(mesh):
    split = (P("ctx", "tp"), P(("ctx", "tp"), None), P(("ctx", "tp"), None), P("ctx", "tp"))
    return jax.shard_map(
        shards, mesh=mesh, in_specs=split, out_specs=split[:3], check_vma=False
    )
```

```python
import math

import jax
import jax.numpy as jnp
from jax import lax
from jax.experimental import pallas as pl
from jax.experimental.pallas import tpu as pltpu
from jax.sharding import PartitionSpec as P

F32 = jnp.float32
BF16 = jnp.bfloat16
MESH = pl.DeviceIdType.MESH
EPS = 1e-6
D = 128
HEADS = 8
ROWS = 1024
BLOCK = 256
HALF = BLOCK // 2
LINE = 16
INV = 1.0 / math.sqrt(D)
EXP2 = INV * math.log2(math.e)
KEYS, VALUES = 0, 1

ORDER = (
    ((0, 0),),
    ((1, 0), (3, 0), (0, 1), (0, 3)),
    ((1, 1), (1, 3), (3, 1), (3, 3)),
    ((2, 0), (0, 2)),
    ((1, 2), (3, 2), (2, 1), (2, 3)),
    ((2, 2),),
)
PLACE = {at: n for n, at in enumerate(sum(ORDER, ()))}
GROUPS = [(PLACE[group[0]], PLACE[group[-1]] + 1) for group in ORDER]
FAR_FIRST = (8, 7, 9, 6, 10, 5, 11, 4, 12, 3, 13, 2, 14, 15, 1)

G_FIRST = 1
G_SECOND = 4
R_FIRST = 1
R_SECOND = 0


def unit(raw):
    scale = lax.rsqrt(jnp.mean(raw * raw, axis=-1, keepdims=True) + EPS)
    return raw * scale, scale


def unit_back(grad, unit_rows, scale):
    return scale * (grad - unit_rows * jnp.mean(grad * unit_rows, axis=-1, keepdims=True))


def place(kind, a, b):
    a, b = a % 4, b % 4
    return PLACE[(a, b) if kind == KEYS else (b, a)]


def rows_of(half):
    return slice(0, BLOCK) if half is None else slice(half * HALF, (half + 1) * HALF)


def kernel(
    q_in, k_in, v_in, do_in,
    gq_ref, gk_ref, gv_ref,
    q_ref, k_ref, v_ref, do_ref, q_t, do_t, q_n, do_n, raised, dots, totals, weighted, rows, dq_t,
    mine, kv, part, piece_in, full_in, last_piece, last_full, line_in,
    load, z_sem, y_sem, send, recv, r_send, p_recv, f_recv, l_recv,
):
    ctx = lax.axis_index("ctx")
    tp = lax.axis_index("tp")
    y, z_hi, x = ctx // 8, (ctx // 4) % 2, ctx % 4
    me = z_hi * 8 + tp

    def beside(kind, axis, step):
        if axis == kind:
            return (y * 8 + z_hi * 4 + (x + step) % 4, tp)
        return (((y + step) % 4) * 8 + z_hi * 4 + x, tp)

    def on_line(step):
        other = (me + step) % LINE
        return (y * 8 + (other // 8) * 4 + x, other % 8)

    def take(ref, sem):
        pltpu.make_async_copy(ref, ref, sem).wait()

    barrier = pltpu.get_barrier_semaphore()
    for step in FAR_FIRST:
        pl.semaphore_signal(barrier, inc=1, device_id=on_line(step), device_id_type=MESH)
    for axis in range(2):
        for step in (1, 2, 3):
            pl.semaphore_signal(barrier, inc=1, device_id=beside(KEYS, axis, step), device_id_type=MESH)

    loads = [
        pltpu.make_async_copy(source, target, load.at[n])
        for n, (source, target) in enumerate(((k_in, k_ref), (v_in, v_ref), (q_in, q_ref), (do_in, do_ref)))
    ]
    for copy in loads:
        copy.start()
    totals[...] = jnp.zeros_like(totals)
    weighted[...] = jnp.zeros_like(weighted)
    dq_t[...] = jnp.zeros_like(dq_t)
    loads[0].wait()
    loads[1].wait()
    for h in range(HEADS):
        cols = slice(h * D, (h + 1) * D)
        mine[h, KEYS] = unit(k_ref[:, cols].astype(F32))[0].astype(BF16)
        mine[h, VALUES] = v_ref[:, cols]
    pl.semaphore_wait(barrier, LINE - 1 + 6)

    for step in FAR_FIRST:
        target = on_line(step)
        pltpu.make_async_remote_copy(
            src_ref=mine.at[target[1]],
            dst_ref=kv.at[0, :, pl.ds((LINE - step) * 16, 16), :],
            send_sem=z_sem.at[0],
            recv_sem=z_sem.at[1],
            device_id=target,
            device_id_type=MESH,
        ).start()
    kv[0, :, 0:16, :] = mine[tp]

    loads[2].wait()
    loads[3].wait()
    for h in range(HEADS):
        cols = slice(h * D, (h + 1) * D)
        cast = unit(q_ref[:, cols].astype(F32))[0].astype(BF16)
        q_n[cols, :] = cast
        q_t[:, cols] = cast.T
        do_n[cols, :] = do_ref[:, cols]
        do_t[:, cols] = do_ref[:, cols].T

    others = kv.at[0, :, 16:BLOCK, :]
    take(others, z_sem.at[1])

    def forward(a, b, axis, step, half=None):
        for kind in range(2):
            src = place(kind, a, b)
            to = ((a - step) % 4, b) if axis == 0 else (a, (b - step) % 4)
            pltpu.make_async_remote_copy(
                src_ref=kv.at[src, kind, rows_of(half), :],
                dst_ref=kv.at[place(kind, *to), kind, rows_of(half), :],
                send_sem=send,
                recv_sem=recv.at[to],
                device_id=beside(kind, axis, step % 4),
                device_id_type=MESH,
            ).start()

    def straight(a):
        return G_SECOND >> a & 1

    def out_second(a):
        for step in (1, -1) + ((2,) if straight(a) else ()):
            forward(a, 0, 1, step)

    def got(a, b):
        take(kv.at[0], recv.at[a, b])
        if b in (1, 3) and not straight(a):
            forward(a, b, 1, b - 2, half=1 if b == 1 else 0)
        if b == 0 and a in (1, 3) and not G_FIRST:
            forward(a, 0, 0, a - 2, half=1 if a == 1 else 0)

    def run(body, group):
        lax.fori_loop(*GROUPS[group], body, 0)

    def pass_1(n, carry):
        scores = jnp.dot(kv[n, KEYS], q_t[...], preferred_element_type=F32)
        value_dots = jnp.dot(kv[n, VALUES], do_t[...], preferred_element_type=F32)
        e = jnp.exp2(scores * EXP2)
        raised[n] = e
        dots[n] = value_dots
        totals[...] += jnp.sum(e.reshape(BLOCK // 8, 8, ROWS), axis=0)
        weighted[...] += jnp.sum((e * value_dots).reshape(BLOCK // 8, 8, ROWS), axis=0)
        return carry

    for step in (1, -1) + ((2,) if G_FIRST else ()):
        forward(0, 0, 0, step)
    out_second(0)
    def block(body, *at):
        for one in at:
            n = PLACE[one]
            lax.fori_loop(n, n + 1, body, 0)

    run(pass_1, 0)
    got(1, 0)
    out_second(1)
    got(3, 0)
    out_second(3)
    got(2, 0)
    out_second(2)
    got(0, 1)
    got(0, 3)
    run(pass_1, 1)
    got(1, 1)
    got(1, 3)
    got(3, 1)
    got(3, 3)
    run(pass_1, 2)
    got(0, 2)
    got(2, 1)
    got(2, 3)
    run(pass_1, 3)
    got(1, 2)
    block(pass_1, (1, 2), (2, 1))
    got(3, 2)
    block(pass_1, (3, 2), (2, 3))
    got(2, 2)
    run(pass_1, 5)
    total = jnp.sum(totals[...], axis=0, keepdims=True)
    inverse = 1.0 / total
    rows[0:1, :] = inverse
    rows[1:2, :] = jnp.sum(weighted[...], axis=0, keepdims=True) * inverse

    def pass_2(n, carry):
        attend = raised[n] * rows[0:1, :]
        score_grad = (attend * (dots[n] - rows[1:2, :])).astype(BF16)
        part[n, VALUES] = jnp.dot(attend.astype(BF16), do_n[...], preferred_element_type=F32).astype(BF16)
        part[n, KEYS] = (jnp.dot(score_grad, q_n[...], preferred_element_type=F32) * INV).astype(BF16)
        dq_t[...] += jnp.dot(kv[n, KEYS].T, score_grad, preferred_element_type=F32)
        return carry

    def give(src, dst, sem, kind, axis, step):
        pltpu.make_async_remote_copy(
            src_ref=src,
            dst_ref=dst,
            send_sem=r_send,
            recv_sem=sem,
            device_id=beside(kind, axis, step % 4),
            device_id_type=MESH,
        ).start()

    def add(kind, at, half, *refs):
        where = (at, kind, rows_of(half), slice(None))
        value = part[where].astype(F32)
        for ref in refs:
            value = value + ref[...].astype(F32)
        part[where] = value.astype(BF16)

    def buffers(a, axis):
        if axis == 1:
            return (piece_in.at[a], p_recv.at[a], full_in.at[a], f_recv.at[a], R_SECOND >> a & 1)
        return (last_piece, l_recv, last_full, l_recv.at[2], R_FIRST)

    def far(a, b, axis, kinds=(KEYS, VALUES)):
        pieces, p_sems, fulls, f_sem, direct = buffers(a, axis)
        for kind in kinds:
            at = place(kind, a, b)
            if direct:
                give(part.at[at, kind], fulls.at[kind, 2], f_sem, kind, axis, 2)
                continue
            for half, step in ((0, 1), (1, -1)):
                give(part.at[at, kind, rows_of(half), :], pieces.at[kind, half], p_sems.at[half], kind, axis, step)

    def near(a, b, axis):
        pieces, p_sems, fulls, f_sem, direct = buffers(a, axis)
        step = 2 - (a if axis == 0 else b)
        half = 0 if step == 1 else 1
        if not direct:
            take(kv.at[0, 0], p_sems.at[half])
        for kind in range(2):
            at = place(kind, a, b)
            if not direct:
                add(kind, at, half, pieces.at[kind, half])
            give(part.at[at, kind], fulls.at[kind, half], f_sem, kind, axis, step)

    def own(a, axis):
        pieces, p_sems, fulls, f_sem, direct = buffers(a, axis)
        sides = 3 if direct else 2
        take(kv.at[0:sides], f_sem)
        for kind in range(2):
            add(kind, place(kind, a, 0), None, *[fulls.at[kind, side] for side in range(sides)])

    K1, V1 = (KEYS,), (VALUES,)
    block(pass_2, (2, 2))
    far(2, 2, 1)
    block(pass_2, (1, 2))
    far(1, 2, 1, K1)
    block(pass_2, (3, 2))
    far(3, 2, 1, K1)
    block(pass_2, (2, 1))
    far(1, 2, 1, V1)
    block(pass_2, (2, 3))
    far(3, 2, 1, V1)
    block(pass_2, (0, 2))
    far(0, 2, 1, K1)
    block(pass_2, (2, 0))
    far(0, 2, 1, V1)
    near(2, 1, 1)
    block(pass_2, (1, 1))
    near(2, 3, 1)
    block(pass_2, (1, 3))
    near(1, 1, 1)
    block(pass_2, (3, 1))
    near(1, 3, 1)
    near(3, 1, 1)
    block(pass_2, (3, 3))
    near(3, 3, 1)
    block(pass_2, (1, 0), (3, 0))
    own(2, 1)
    far(2, 0, 0)
    block(pass_2, (0, 1), (0, 3))
    near(0, 1, 1)
    near(0, 3, 1)
    block(pass_2, (0, 0))
    for a in (1, 3):
        own(a, 1)
        near(a, 0, 0)

    for h in range(HEADS):
        cols = slice(h * D, (h + 1) * D)
        unit_rows, scale = unit(q_ref[:, cols].astype(F32))
        gq_ref[:, cols] = unit_back(dq_t[:, cols].T * INV, unit_rows, scale).astype(BF16)

    own(0, 1)
    own(0, 0)

    for step in FAR_FIRST:
        pltpu.make_async_remote_copy(
            src_ref=part.at[0, :, pl.ds(step * 16, 16), :],
            dst_ref=line_in.at[me],
            send_sem=y_sem.at[0],
            recv_sem=y_sem.at[1],
            device_id=on_line(step),
            device_id_type=MESH,
        ).start()
    line_in[me] = part[0, :, 0:16, :]
    take(others, z_sem.at[0])
    take(kv.at[0:15], send)
    take(part.at[0:15], r_send)
    take(line_in.at[0 : LINE - 1], y_sem.at[1])
    for h in range(HEADS):
        cols = slice(h * D, (h + 1) * D)
        sums = line_in[h].astype(F32) + line_in[h + 8].astype(F32)
        unit_rows, scale = unit(k_ref[:, cols].astype(F32))
        gk_ref[:, cols] = unit_back(sums[KEYS], unit_rows, scale).astype(BF16)
        gv_ref[:, cols] = sums[VALUES].astype(BF16)
    take(line_in.at[0 : LINE - 1], y_sem.at[0])


def hand_over(*refs):
    for source, target in zip(refs[:3], refs[3:]):
        target[...] = source[...]


def shards(query_raw, key_raw, values, grad_out):
    vmem = pl.BlockSpec(memory_space=pltpu.VMEM)
    anywhere = pl.BlockSpec(memory_space=pl.ANY)
    dma = pltpu.SemaphoreType.DMA
    outs = [jax.ShapeDtypeStruct(a.shape, BF16) for a in (query_raw, key_raw, values)]
    grads = pl.pallas_call(
        kernel,
        out_shape=outs,
        in_specs=[anywhere] * 4,
        out_specs=[vmem] * 3,
        scratch_shapes=[
            pltpu.VMEM((D, ROWS), BF16),
            pltpu.VMEM((16, ROWS), BF16),
            pltpu.VMEM((16, ROWS), BF16),
            pltpu.VMEM((D, ROWS), BF16),
            pltpu.VMEM((D, ROWS), BF16),
            pltpu.VMEM((D, ROWS), BF16),
            pltpu.VMEM((ROWS, D), BF16),
            pltpu.VMEM((ROWS, D), BF16),
            pltpu.VMEM((16, BLOCK, ROWS), F32),
            pltpu.VMEM((16, BLOCK, ROWS), F32),
            pltpu.VMEM((8, ROWS), F32),
            pltpu.VMEM((8, ROWS), F32),
            pltpu.VMEM((8, ROWS), F32),
            pltpu.VMEM((D, ROWS), F32),
            pltpu.VMEM((HEADS, 2, 16, D), BF16),
            pltpu.VMEM((16, 2, BLOCK, D), BF16),
            pltpu.VMEM((16, 2, BLOCK, D), BF16),
            pltpu.VMEM((4, 2, 2, HALF, D), BF16),
            pltpu.VMEM((4, 2, 3, BLOCK, D), BF16),
            pltpu.VMEM((2, 2, HALF, D), BF16),
            pltpu.VMEM((2, 3, BLOCK, D), BF16),
            pltpu.VMEM((LINE, 2, 16, D), BF16),
            dma((4,)),
            dma((2,)),
            dma((2,)),
            dma,
            dma((4, 4)),
            dma,
            dma((4, 2)),
            dma((4,)),
            dma((3,)),
        ],
        compiler_params=pltpu.CompilerParams(
            collective_id=0, has_side_effects=True, vmem_limit_bytes=56 * 2**20
        ),
    )(query_raw, key_raw, values, grad_out)
    return pl.pallas_call(hand_over, out_shape=outs, in_specs=[vmem] * 3, out_specs=[vmem] * 3)(*grads)


def solution(mesh):
    split = (P("ctx", "tp"), P(("ctx", "tp"), None), P(("ctx", "tp"), None), P("ctx", "tp"))
    return jax.shard_map(
        shards, mesh=mesh, in_specs=split, out_specs=split[:3], check_vma=False
    )
```

```python
import math

import jax
import jax.numpy as jnp
from jax import lax
from jax.experimental import pallas as pl
from jax.experimental.pallas import tpu as pltpu
from jax.sharding import PartitionSpec as P

F32 = jnp.float32
BF16 = jnp.bfloat16
MESH = pl.DeviceIdType.MESH
EPS = 1e-6
D = 128
HEADS = 8
ROWS = 1024
BLOCK = 256
HALF = BLOCK // 2
LINE = 16
INV = 1.0 / math.sqrt(D)
EXP2 = INV * math.log2(math.e)
KEYS, VALUES = 0, 1

ORDER = (
    ((0, 0),),
    ((1, 0), (3, 0), (0, 1), (0, 3)),
    ((1, 1), (1, 3), (3, 1), (3, 3)),
    ((2, 0), (0, 2)),
    ((1, 2), (3, 2), (2, 1), (2, 3)),
    ((2, 2),),
)
PLACE = {at: n for n, at in enumerate(sum(ORDER, ()))}
GROUPS = [(PLACE[group[0]], PLACE[group[-1]] + 1) for group in ORDER]
FAR_FIRST = (8, 7, 9, 6, 10, 5, 11, 4, 12, 3, 13, 2, 14, 15, 1)

G_FIRST = 1
G_SECOND = 4
R_FIRST = 1
R_SECOND = 0


def unit(raw):
    scale = lax.rsqrt(jnp.mean(raw * raw, axis=-1, keepdims=True) + EPS)
    return raw * scale, scale


def unit_back(grad, unit_rows, scale):
    return scale * (grad - unit_rows * jnp.mean(grad * unit_rows, axis=-1, keepdims=True))


def place(kind, a, b):
    a, b = a % 4, b % 4
    return PLACE[(a, b) if kind == KEYS else (b, a)]


def rows_of(half):
    return slice(0, BLOCK) if half is None else slice(half * HALF, (half + 1) * HALF)


def kernel(
    q_in, k_in, v_in, do_in,
    gq_ref, gk_ref, gv_ref,
    q_ref, k_ref, v_ref, do_ref, q_t, do_t, q_n, do_n, raised, dots, totals, weighted, rows, dq_t,
    mine, kv, part, piece_in, full_in, last_piece, last_full, line_in,
    load, z_sem, y_sem, send, recv, r_send, p_recv, f_recv, l_recv,
):
    ctx = lax.axis_index("ctx")
    tp = lax.axis_index("tp")
    y, z_hi, x = ctx // 8, (ctx // 4) % 2, ctx % 4
    me = z_hi * 8 + tp

    def beside(kind, axis, step):
        if axis == kind:
            return (y * 8 + z_hi * 4 + (x + step) % 4, tp)
        return (((y + step) % 4) * 8 + z_hi * 4 + x, tp)

    def on_line(step):
        other = (me + step) % LINE
        return (y * 8 + (other // 8) * 4 + x, other % 8)

    def take(ref, sem):
        pltpu.make_async_copy(ref, ref, sem).wait()

    barrier = pltpu.get_barrier_semaphore()
    for step in FAR_FIRST:
        pl.semaphore_signal(barrier, inc=1, device_id=on_line(step), device_id_type=MESH)
    for axis in range(2):
        for step in (1, 2, 3):
            pl.semaphore_signal(barrier, inc=1, device_id=beside(KEYS, axis, step), device_id_type=MESH)

    loads = [
        pltpu.make_async_copy(source, target, load.at[n])
        for n, (source, target) in enumerate(((k_in, k_ref), (v_in, v_ref), (q_in, q_ref), (do_in, do_ref)))
    ]
    for copy in loads:
        copy.start()
    totals[...] = jnp.zeros_like(totals)
    weighted[...] = jnp.zeros_like(weighted)
    dq_t[...] = jnp.zeros_like(dq_t)
    loads[0].wait()
    loads[1].wait()
    for h in range(HEADS):
        cols = slice(h * D, (h + 1) * D)
        mine[h, KEYS] = unit(k_ref[:, cols].astype(F32))[0].astype(BF16)
        mine[h, VALUES] = v_ref[:, cols]
    pl.semaphore_wait(barrier, LINE - 1 + 6)

    for step in FAR_FIRST:
        target = on_line(step)
        pltpu.make_async_remote_copy(
            src_ref=mine.at[target[1]],
            dst_ref=kv.at[0, :, pl.ds((LINE - step) * 16, 16), :],
            send_sem=z_sem.at[0],
            recv_sem=z_sem.at[1],
            device_id=target,
            device_id_type=MESH,
        ).start()
    kv[0, :, 0:16, :] = mine[tp]

    loads[2].wait()
    loads[3].wait()
    for h in range(HEADS):
        cols = slice(h * D, (h + 1) * D)
        cast = unit(q_ref[:, cols].astype(F32))[0].astype(BF16)
        q_n[cols, :] = cast
        q_t[:, cols] = cast.T
        do_n[cols, :] = do_ref[:, cols]
        do_t[:, cols] = do_ref[:, cols].T

    others = kv.at[0, :, 16:BLOCK, :]
    take(others, z_sem.at[1])

    def forward(a, b, axis, step, half=None):
        for kind in range(2):
            src = place(kind, a, b)
            to = ((a - step) % 4, b) if axis == 0 else (a, (b - step) % 4)
            pltpu.make_async_remote_copy(
                src_ref=kv.at[src, kind, rows_of(half), :],
                dst_ref=kv.at[place(kind, *to), kind, rows_of(half), :],
                send_sem=send,
                recv_sem=recv.at[to],
                device_id=beside(kind, axis, step % 4),
                device_id_type=MESH,
            ).start()

    def straight(a):
        return G_SECOND >> a & 1

    def out_second(a):
        for step in (1, -1) + ((2,) if straight(a) else ()):
            forward(a, 0, 1, step)

    def got(a, b):
        take(kv.at[0], recv.at[a, b])
        if b in (1, 3) and not straight(a):
            forward(a, b, 1, b - 2, half=1 if b == 1 else 0)
        if b == 0 and a in (1, 3) and not G_FIRST:
            forward(a, 0, 0, a - 2, half=1 if a == 1 else 0)

    def run(body, group):
        lax.fori_loop(*GROUPS[group], body, 0)

    def pass_1(n, carry):
        scores = jnp.dot(kv[n, KEYS], q_t[...], preferred_element_type=F32)
        value_dots = jnp.dot(kv[n, VALUES], do_t[...], preferred_element_type=F32)
        e = jnp.exp2(scores * EXP2)
        raised[n] = e
        dots[n] = value_dots
        totals[...] += jnp.sum(e.reshape(BLOCK // 8, 8, ROWS), axis=0)
        weighted[...] += jnp.sum((e * value_dots).reshape(BLOCK // 8, 8, ROWS), axis=0)
        return carry

    for step in (1, -1) + ((2,) if G_FIRST else ()):
        forward(0, 0, 0, step)
    out_second(0)
    def block(body, *at):
        for one in at:
            n = PLACE[one]
            lax.fori_loop(n, n + 1, body, 0)

    run(pass_1, 0)
    got(1, 0)
    out_second(1)
    got(3, 0)
    out_second(3)
    got(2, 0)
    out_second(2)
    got(0, 1)
    got(0, 3)
    run(pass_1, 1)
    got(1, 1)
    got(1, 3)
    got(3, 1)
    got(3, 3)
    run(pass_1, 2)
    got(0, 2)
    got(2, 1)
    got(2, 3)
    run(pass_1, 3)
    got(1, 2)
    block(pass_1, (1, 2), (2, 1))
    got(3, 2)
    block(pass_1, (3, 2), (2, 3))
    got(2, 2)
    run(pass_1, 5)
    total = jnp.sum(totals[...], axis=0, keepdims=True)
    inverse = 1.0 / total
    rows[0:1, :] = inverse
    rows[1:2, :] = jnp.sum(weighted[...], axis=0, keepdims=True) * inverse

    def pass_2(n, carry):
        attend = raised[n] * rows[0:1, :]
        score_grad = (attend * (dots[n] - rows[1:2, :])).astype(BF16)
        part[n, VALUES] = jnp.dot(attend.astype(BF16), do_n[...], preferred_element_type=F32).astype(BF16)
        part[n, KEYS] = (jnp.dot(score_grad, q_n[...], preferred_element_type=F32) * INV).astype(BF16)
        dq_t[...] += jnp.dot(kv[n, KEYS].T, score_grad, preferred_element_type=F32)
        return carry

    def give(src, dst, sem, kind, axis, step):
        pltpu.make_async_remote_copy(
            src_ref=src,
            dst_ref=dst,
            send_sem=r_send,
            recv_sem=sem,
            device_id=beside(kind, axis, step % 4),
            device_id_type=MESH,
        ).start()

    def add(kind, at, half, *refs):
        where = (at, kind, rows_of(half), slice(None))
        value = part[where].astype(F32)
        for ref in refs:
            value = value + ref[...].astype(F32)
        part[where] = value.astype(BF16)

    def buffers(a, axis):
        if axis == 1:
            return (piece_in.at[a], p_recv.at[a], full_in.at[a], f_recv.at[a], R_SECOND >> a & 1)
        return (last_piece, l_recv, last_full, l_recv.at[2], R_FIRST)

    def far(a, b, axis, kinds=(KEYS, VALUES)):
        pieces, p_sems, fulls, f_sem, direct = buffers(a, axis)
        for kind in kinds:
            at = place(kind, a, b)
            if direct:
                give(part.at[at, kind], fulls.at[kind, 2], f_sem, kind, axis, 2)
                continue
            for half, step in ((0, 1), (1, -1)):
                give(part.at[at, kind, rows_of(half), :], pieces.at[kind, half], p_sems.at[half], kind, axis, step)

    def near(a, b, axis):
        pieces, p_sems, fulls, f_sem, direct = buffers(a, axis)
        step = 2 - (a if axis == 0 else b)
        half = 0 if step == 1 else 1
        if not direct:
            take(kv.at[0, 0], p_sems.at[half])
        for kind in range(2):
            at = place(kind, a, b)
            if not direct:
                add(kind, at, half, pieces.at[kind, half])
            give(part.at[at, kind], fulls.at[kind, half], f_sem, kind, axis, step)

    def own(a, axis):
        pieces, p_sems, fulls, f_sem, direct = buffers(a, axis)
        sides = 3 if direct else 2
        take(kv.at[0:sides], f_sem)
        for kind in range(2):
            add(kind, place(kind, a, 0), None, *[fulls.at[kind, side] for side in range(sides)])

    K1, V1 = (KEYS,), (VALUES,)
    block(pass_2, (2, 2))
    far(2, 2, 1)
    block(pass_2, (1, 2))
    far(1, 2, 1, K1)
    block(pass_2, (3, 2))
    far(3, 2, 1, K1)
    block(pass_2, (2, 1))
    far(1, 2, 1, V1)
    block(pass_2, (2, 3))
    far(3, 2, 1, V1)
    block(pass_2, (0, 2))
    far(0, 2, 1, K1)
    block(pass_2, (2, 0))
    far(0, 2, 1, V1)
    near(2, 1, 1)
    block(pass_2, (1, 1))
    near(2, 3, 1)
    block(pass_2, (1, 3))
    near(1, 1, 1)
    block(pass_2, (3, 1))
    near(1, 3, 1)
    near(3, 1, 1)
    block(pass_2, (3, 3))
    near(3, 3, 1)
    block(pass_2, (1, 0), (3, 0))
    own(2, 1)
    far(2, 0, 0)
    block(pass_2, (0, 1), (0, 3))
    near(0, 1, 1)
    near(0, 3, 1)
    block(pass_2, (0, 0))
    for a in (1, 3):
        own(a, 1)
        near(a, 0, 0)

    for h in range(HEADS):
        cols = slice(h * D, (h + 1) * D)
        unit_rows, scale = unit(q_ref[:, cols].astype(F32))
        gq_ref[:, cols] = unit_back(dq_t[:, cols].T * INV, unit_rows, scale).astype(BF16)

    own(0, 1)
    own(0, 0)

    for step in FAR_FIRST:
        pltpu.make_async_remote_copy(
            src_ref=part.at[0, :, pl.ds(step * 16, 16), :],
            dst_ref=line_in.at[me],
            send_sem=y_sem.at[0],
            recv_sem=y_sem.at[1],
            device_id=on_line(step),
            device_id_type=MESH,
        ).start()
    line_in[me] = part[0, :, 0:16, :]
    take(others, z_sem.at[0])
    take(kv.at[0:15], send)
    take(part.at[0:15], r_send)
    take(line_in.at[0 : LINE - 1], y_sem.at[1])
    for h in range(HEADS):
        cols = slice(h * D, (h + 1) * D)
        sums = line_in[h].astype(F32) + line_in[h + 8].astype(F32)
        unit_rows, scale = unit(k_ref[:, cols].astype(F32))
        gk_ref[:, cols] = unit_back(sums[KEYS], unit_rows, scale).astype(BF16)
        gv_ref[:, cols] = sums[VALUES].astype(BF16)
    take(line_in.at[0 : LINE - 1], y_sem.at[0])


def hand_over(*refs):
    for source, target in zip(refs[:3], refs[3:]):
        target[...] = source[...]


def shards(query_raw, key_raw, values, grad_out):
    vmem = pl.BlockSpec(memory_space=pltpu.VMEM)
    anywhere = pl.BlockSpec(memory_space=pl.ANY)
    dma = pltpu.SemaphoreType.DMA
    outs = [jax.ShapeDtypeStruct(a.shape, BF16) for a in (query_raw, key_raw, values)]
    grads = pl.pallas_call(
        kernel,
        out_shape=[pltpu.VMEM(a.shape, a.dtype) for a in outs],
        in_specs=[anywhere] * 4,
        out_specs=[vmem] * 3,
        scratch_shapes=[
            pltpu.VMEM((D, ROWS), BF16),
            pltpu.VMEM((16, ROWS), BF16),
            pltpu.VMEM((16, ROWS), BF16),
            pltpu.VMEM((D, ROWS), BF16),
            pltpu.VMEM((D, ROWS), BF16),
            pltpu.VMEM((D, ROWS), BF16),
            pltpu.VMEM((ROWS, D), BF16),
            pltpu.VMEM((ROWS, D), BF16),
            pltpu.VMEM((16, BLOCK, ROWS), F32),
            pltpu.VMEM((16, BLOCK, ROWS), F32),
            pltpu.VMEM((8, ROWS), F32),
            pltpu.VMEM((8, ROWS), F32),
            pltpu.VMEM((8, ROWS), F32),
            pltpu.VMEM((D, ROWS), F32),
            pltpu.VMEM((HEADS, 2, 16, D), BF16),
            pltpu.VMEM((16, 2, BLOCK, D), BF16),
            pltpu.VMEM((16, 2, BLOCK, D), BF16),
            pltpu.VMEM((4, 2, 2, HALF, D), BF16),
            pltpu.VMEM((4, 2, 3, BLOCK, D), BF16),
            pltpu.VMEM((2, 2, HALF, D), BF16),
            pltpu.VMEM((2, 3, BLOCK, D), BF16),
            pltpu.VMEM((LINE, 2, 16, D), BF16),
            dma((4,)),
            dma((2,)),
            dma((2,)),
            dma,
            dma((4, 4)),
            dma,
            dma((4, 2)),
            dma((4,)),
            dma((3,)),
        ],
        compiler_params=pltpu.CompilerParams(
            collective_id=0, has_side_effects=True, vmem_limit_bytes=56 * 2**20
        ),
    )(query_raw, key_raw, values, grad_out)
    return pl.pallas_call(hand_over, out_shape=outs, in_specs=[vmem] * 3, out_specs=[vmem] * 3)(
        *[pltpu.with_memory_space_constraint(grad, pltpu.VMEM) for grad in grads]
    )


def solution(mesh):
    split = (P("ctx", "tp"), P(("ctx", "tp"), None), P(("ctx", "tp"), None), P("ctx", "tp"))
    return jax.shard_map(
        shards, mesh=mesh, in_specs=split, out_specs=split[:3], check_vma=False
    )
```

```python
import math

import jax
import jax.numpy as jnp
from jax import lax
from jax.experimental import pallas as pl
from jax.experimental.pallas import tpu as pltpu
from jax.sharding import PartitionSpec as P

F32 = jnp.float32
BF16 = jnp.bfloat16
MESH = pl.DeviceIdType.MESH
EPS = 1e-6
D = 128
HEADS = 8
ROWS = 1024
BLOCK = 256
LINE = 16
INV = 1.0 / math.sqrt(D)
EXP2 = INV * math.log2(math.e)
KEYS, VALUES = 0, 1

BLOCKS = ((0, 0), (0, 3), (0, 1), (0, 2), (1, 0), (1, 3), (1, 1), (1, 2))
PLACE = {at: n for n, at in enumerate(BLOCKS)}
LINES = [(1, dz) for dz in (4, 3, 5, 2, 6, 1, 7, 0)] + [(0, dz) for dz in (4, 3, 5, 2, 6, 1, 7)]
LATE = 1


def unit(raw):
    scale = lax.rsqrt(jnp.mean(raw * raw, axis=-1, keepdims=True) + EPS)
    return raw * scale, scale


def unit_back(grad, unit_rows, scale):
    return scale * (grad - unit_rows * jnp.mean(grad * unit_rows, axis=-1, keepdims=True))


def kernel(
    q_in, k_in, v_in, do_in,
    gq_ref, gk_ref, gv_ref,
    q_ref, k_ref, v_ref, do_ref, q_t, do_t, q_n, do_n, raised, dots, totals, weighted, rows, dq_t,
    mine, kv, part, sib_in, y_in, x_in, line_in, gq_out, gq_in,
    load, swap, z_sem, l_sem, send, recv, s_send, s_recv, t_send, t_recv, r_send, yr_recv, xr_recv, back,
):
    ctx = lax.axis_index("ctx")
    tp = lax.axis_index("tp")
    y, x = ctx // 8, ctx % 4
    z = ((ctx // 4) % 2) * 4 + tp // 2
    core = tp % 2
    group = x // 2
    stays = core == group
    def device(at_x, at_y, at_z, at_core):
        at_z = at_z % 8
        return ((at_y % 4) * 8 + (at_z // 4) * 4 + at_x % 4, (at_z % 4) * 2 + at_core)

    beside_x = device(x + 1 - 2 * (x % 2), y, z, core)
    sibling = device(x, y, z, 1 - core)
    partner = device(x + 2, y, z, 1 - core)

    def beside_y(step):
        return device(x, y + step + 4, z, core)

    def on_line(l, dz):
        return device(x + 2 * l, y, z + dz, core)

    def copy_to(src, dst, send_sem, recv_sem, target):
        pltpu.make_async_remote_copy(
            src_ref=src, dst_ref=dst, send_sem=send_sem, recv_sem=recv_sem, device_id=target, device_id_type=MESH
        ).start()

    def take(ref, sem):
        pltpu.make_async_copy(ref, ref, sem).wait()

    barrier = pltpu.get_barrier_semaphore()
    greeted = [on_line(l, dz) for l, dz in LINES] + [beside_y(step) for step in (1, 2, 3)]
    greeted += [beside_x, sibling, partner]
    for target in greeted:
        pl.semaphore_signal(barrier, inc=1, device_id=target, device_id_type=MESH)
    k_load = pltpu.make_async_copy(k_in, k_ref, load.at[0])
    v_load = pltpu.make_async_copy(v_in, v_ref, load.at[1])
    k_load.start()
    v_load.start()

    @pl.when(stays)
    def _():
        pltpu.make_async_copy(q_in, q_ref, swap.at[1]).start()
        pltpu.make_async_copy(do_in, do_ref, swap.at[2]).start()

    totals[...] = jnp.zeros_like(totals)
    weighted[...] = jnp.zeros_like(weighted)
    dq_t[...] = jnp.zeros_like(dq_t)
    k_load.wait()
    v_load.wait()
    for h in range(HEADS):
        cols = slice(h * D, (h + 1) * D)
        mine[h, KEYS] = unit(k_ref[:, cols].astype(F32))[0].astype(BF16)
        mine[h, VALUES] = v_ref[:, cols]
    pl.semaphore_wait(barrier, len(greeted))

    for l, dz in LINES:
        head = 2 * ((z + dz) % 4) + ((x + 2 * l) % 4) // 2
        spot = (l * 8 + (8 - dz) % 8) * 16
        copy_to(mine.at[head], kv.at[0, :, spot : spot + 16, :], z_sem.at[0], z_sem.at[1], on_line(l, dz))
    kv[0, :, 0:16, :] = mine[2 * (z % 4) + group]

    @pl.when(jnp.logical_not(stays))
    def _():
        copy_to(q_in, q_ref, swap.at[0], swap.at[1], partner)
        copy_to(do_in, do_ref, swap.at[3], swap.at[2], partner)

    others = kv.at[0, :, 16:BLOCK, :]
    take(others, z_sem.at[1])

    def along_x(kind, i, b):
        to = PLACE[1 - i, b]
        copy_to(kv.at[2 * PLACE[i, b], kind], kv.at[2 * to, kind], send, recv.at[kind, to], beside_x)

    def along_y(kind, i, b):
        for step in (1, 3, 2):
            to = PLACE[i, (b - step) % 4]
            copy_to(kv.at[2 * PLACE[i, b], kind], kv.at[2 * to, kind], send, recv.at[kind, to], beside_y(step))

    def got(kind, i, b):
        n = PLACE[i, b]
        take(kv.at[0, 0], recv.at[kind, n])
        if kind == KEYS and b == 0:
            along_y(kind, i, b)
        if kind == VALUES and i == 0:
            along_x(kind, i, b)
        copy_to(kv.at[2 * n, kind], kv.at[2 * n + 1, kind], s_send, s_recv.at[n], sibling)

    along_x(KEYS, 0, 0)
    along_y(VALUES, 0, 0)
    along_y(KEYS, 0, 0)
    along_x(VALUES, 0, 0)
    copy_to(kv.at[0], kv.at[1], s_send, s_recv.at[0], sibling)

    def pass_1(n, carry):
        scores = jnp.dot(kv[n, KEYS], q_t[...], preferred_element_type=F32)
        value_dots = jnp.dot(kv[n, VALUES], do_t[...], preferred_element_type=F32)
        e = jnp.exp2(scores * EXP2)
        raised[n] = e
        dots[n] = value_dots
        totals[...] += jnp.sum(e.reshape(BLOCK // 8, 8, ROWS), axis=0)
        weighted[...] += jnp.sum((e * value_dots).reshape(BLOCK // 8, 8, ROWS), axis=0)
        return carry

    def run(body, low, high):
        lax.fori_loop(low, high, body, 0, unroll=True)

    def shared(i, b):
        take(kv.at[0], s_recv.at[PLACE[i, b]])

    take(q_ref, swap.at[1])
    for h in range(HEADS):
        cols = slice(h * D, (h + 1) * D)
        cast = unit(q_ref[:, cols].astype(F32))[0].astype(BF16)
        q_n[cols, :] = cast
        q_t[:, cols] = cast.T
    got(KEYS, 1, 0)
    for b in (3, 1, 2):
        got(VALUES, 0, b)
    take(do_ref, swap.at[2])
    for h in range(HEADS):
        cols = slice(h * D, (h + 1) * D)
        do_n[cols, :] = do_ref[:, cols]
        do_t[:, cols] = do_ref[:, cols].T
    def fetch(m):
        i, b = BLOCKS[m]
        if (i, b) != (1, 0):
            got(KEYS, i, b)
        if i:
            got(VALUES, i, b)

    run(pass_1, 0, 1)
    fetch(1)
    for m in range(1, 8):
        if m < 7:
            fetch(m + 1)
        shared(*BLOCKS[m - 1])
        run(pass_1, 2 * m - 1, 2 * m + 1)
    shared(*BLOCKS[7])
    run(pass_1, 15, 16)
    total = jnp.sum(totals[...], axis=0, keepdims=True)
    inverse = 1.0 / total
    rows[0:1, :] = inverse
    rows[1:2, :] = jnp.sum(weighted[...], axis=0, keepdims=True) * inverse

    def pass_2(t, carry):
        n = 15 - t
        attend = raised[n] * rows[0:1, :]
        score_grad = (attend * (dots[n] - rows[1:2, :])).astype(BF16)
        part[n, VALUES] = jnp.dot(attend.astype(BF16), do_n[...], preferred_element_type=F32).astype(BF16)
        part[n, KEYS] = (jnp.dot(score_grad, q_n[...], preferred_element_type=F32) * INV).astype(BF16)
        dq_t[...] += jnp.dot(kv[n, KEYS].T, score_grad, preferred_element_type=F32)
        return carry

    def share(m):
        copy_to(part.at[2 * m + 1], sib_in.at[m], t_send, t_recv.at[m], sibling)

    def add(i, b, kind, *refs):
        n = 2 * PLACE[i, b]
        value = part[n, kind].astype(F32)
        for ref in refs:
            value = value + ref[...].astype(F32)
        part[n, kind] = value.astype(BF16)

    def settle(i, b):
        m = PLACE[i, b]
        take(kv.at[0], t_recv.at[m])
        came = [sib_in.at[m, VALUES]]
        if i == 0:
            take(kv.at[0, 0], xr_recv.at[b])
            came.append(x_in.at[b])
        add(i, b, VALUES, *came)
        if i == 1:
            copy_to(part.at[2 * m, VALUES], x_in.at[b], r_send, xr_recv.at[b], beside_x)
        elif b:
            copy_to(part.at[2 * m, VALUES], y_in.at[2, b - 1], r_send, yr_recv.at[2], beside_y(b))
        add(i, b, KEYS, sib_in.at[m, KEYS])
        if b:
            copy_to(part.at[2 * m, KEYS], y_in.at[i, b - 1], r_send, yr_recv.at[i], beside_y(b))

    def gather_y(which, i, kind, *more):
        take(y_in.at[0], yr_recv.at[which])
        add(i, 0, kind, y_in.at[which, 0], y_in.at[which, 1], y_in.at[which, 2], *more)

    run(pass_2, 0, 1)
    share(7)
    for m in range(6, -1, -1):
        run(pass_2, 13 - 2 * m, 15 - 2 * m)
        share(m)
        settle(*BLOCKS[m + 1])
        if m == LATE:
            gather_y(1, 1, KEYS)
            copy_to(part.at[2 * PLACE[1, 0], KEYS], x_in.at[4], r_send, xr_recv.at[4], beside_x)
    run(pass_2, 15, 16)

    for h in range(HEADS):
        cols = slice(h * D, (h + 1) * D)
        unit_rows, scale = unit(q_ref[:, cols].astype(F32))
        gq_out[:, cols] = unit_back(dq_t[:, cols].T * INV, unit_rows, scale).astype(BF16)

    @pl.when(jnp.logical_not(stays))
    def _():
        copy_to(gq_out, gq_in, back.at[0], back.at[1], partner)

    settle(0, 0)
    take(kv.at[0, 0], xr_recv.at[4])
    gather_y(0, 0, KEYS, x_in.at[4])
    gather_y(2, 0, VALUES)

    me = group * 8 + z
    for l, dz in LINES:
        spot = (l * 8 + dz) * 16
        copy_to(part.at[0, :, spot : spot + 16, :], line_in.at[me], l_sem.at[0], l_sem.at[1], on_line(l, dz))
    line_in[me] = part[0, :, 0:16, :]
    take(others, z_sem.at[0])
    take(kv.at[0:7], send)
    take(kv.at[0:8], s_send)
    take(part.at[0:8], t_send)
    take(part.at[0:7], r_send)

    @pl.when(stays)
    def _():
        gq_ref[...] = gq_out[...]

    @pl.when(jnp.logical_not(stays))
    def _():
        take(q_ref, swap.at[0])
        take(do_ref, swap.at[3])
        take(gq_out, back.at[0])
        take(gq_in, back.at[1])
        gq_ref[...] = gq_in[...]

    take(line_in.at[0 : LINE - 1], l_sem.at[1])
    for h in range(HEADS):
        cols = slice(h * D, (h + 1) * D)
        low = (h % 2) * 8 + h // 2
        sums = line_in[low].astype(F32) + line_in[low + 4].astype(F32)
        unit_rows, scale = unit(k_ref[:, cols].astype(F32))
        gk_ref[:, cols] = unit_back(sums[KEYS], unit_rows, scale).astype(BF16)
        gv_ref[:, cols] = sums[VALUES].astype(BF16)
    take(line_in.at[0 : LINE - 1], l_sem.at[0])


def hand_over(*refs):
    for source, target in zip(refs[:3], refs[3:]):
        target[...] = source[...]


def shards(query_raw, key_raw, values, grad_out):
    vmem = pl.BlockSpec(memory_space=pltpu.VMEM)
    anywhere = pl.BlockSpec(memory_space=pl.ANY)
    dma = pltpu.SemaphoreType.DMA
    outs = [jax.ShapeDtypeStruct(a.shape, BF16) for a in (query_raw, key_raw, values)]
    grads = pl.pallas_call(
        kernel,
        out_shape=[pltpu.VMEM(a.shape, a.dtype) for a in outs],
        in_specs=[anywhere] * 4,
        out_specs=[vmem] * 3,
        scratch_shapes=[
            pltpu.VMEM((D, ROWS), BF16),
            pltpu.VMEM((16, ROWS), BF16),
            pltpu.VMEM((16, ROWS), BF16),
            pltpu.VMEM((D, ROWS), BF16),
            pltpu.VMEM((D, ROWS), BF16),
            pltpu.VMEM((D, ROWS), BF16),
            pltpu.VMEM((ROWS, D), BF16),
            pltpu.VMEM((ROWS, D), BF16),
            pltpu.VMEM((16, BLOCK, ROWS), F32),
            pltpu.VMEM((16, BLOCK, ROWS), F32),
            pltpu.VMEM((8, ROWS), F32),
            pltpu.VMEM((8, ROWS), F32),
            pltpu.VMEM((8, ROWS), F32),
            pltpu.VMEM((D, ROWS), F32),
            pltpu.VMEM((HEADS, 2, 16, D), BF16),
            pltpu.VMEM((16, 2, BLOCK, D), BF16),
            pltpu.VMEM((16, 2, BLOCK, D), BF16),
            pltpu.VMEM((8, 2, BLOCK, D), BF16),
            pltpu.VMEM((3, 3, BLOCK, D), BF16),
            pltpu.VMEM((5, BLOCK, D), BF16),
            pltpu.VMEM((LINE, 2, 16, D), BF16),
            pltpu.VMEM((D, ROWS), BF16),
            pltpu.VMEM((D, ROWS), BF16),
            dma((2,)),
            dma((4,)),
            dma((2,)),
            dma((2,)),
            dma,
            dma((2, 8)),
            dma,
            dma((8,)),
            dma,
            dma((8,)),
            dma,
            dma((3,)),
            dma((5,)),
            dma((2,)),
        ],
        compiler_params=pltpu.CompilerParams(
            collective_id=0, has_side_effects=True, vmem_limit_bytes=56 * 2**20
        ),
    )(query_raw, key_raw, values, grad_out)
    return pl.pallas_call(hand_over, out_shape=outs, in_specs=[vmem] * 3, out_specs=[vmem] * 3)(
        *[pltpu.with_memory_space_constraint(grad, pltpu.VMEM) for grad in grads]
    )


def solution(mesh):
    split = (P("ctx", "tp"), P(("ctx", "tp"), None), P(("ctx", "tp"), None), P("ctx", "tp"))
    return jax.shard_map(
        shards, mesh=mesh, in_specs=split, out_specs=split[:3], check_vma=False
    )
```

```python
import math

import jax
import jax.numpy as jnp
from jax import lax
from jax.experimental import pallas as pl
from jax.experimental.pallas import tpu as pltpu
from jax.sharding import PartitionSpec as P

F32 = jnp.float32
BF16 = jnp.bfloat16
MESH = pl.DeviceIdType.MESH
EPS = 1e-6
D = 128
HEADS = 8
ROWS = 1024
BLOCK = 256
LINE = 16
INV = 1.0 / math.sqrt(D)
EXP2 = INV * math.log2(math.e)
KEYS, VALUES = 0, 1


BLOCKS = ((0, 0), (0, 3), (0, 1), (0, 2), (1, 0), (1, 3), (1, 1), (1, 2))
PLACE = {at: n for n, at in enumerate(BLOCKS)}
LINES = [(1, dz) for dz in (4, 3, 5, 2, 6, 1, 7, 0)] + [(0, dz) for dz in (4, 3, 5, 2, 6, 1, 7)]
def unit(raw):
    scale = lax.rsqrt(jnp.mean(raw * raw, axis=-1, keepdims=True) + EPS)
    return raw * scale, scale


def unit_back(grad, unit_rows, scale):
    return scale * (grad - unit_rows * jnp.mean(grad * unit_rows, axis=-1, keepdims=True))


def kernel(
    q_in, k_in, v_in, do_in,
    gq_ref, gk_ref, gv_ref,
    q_ref, k_ref, v_ref, do_ref, q_t, do_t, q_n, do_n, raised, dots, grads, totals, weighted, rows, dq_t,
    k_unit, k_scale, mine, kv, part, sib_in, y_in, x_in, line_in, gq_out, gq_in,
    load, swap, z_sem, l_sem, send, recv, s_send, s_recv, t_send, t_recv, r_send, yr_recv, xr_recv, back,
):
    ctx = lax.axis_index("ctx")
    tp = lax.axis_index("tp")
    y, x = ctx // 8, ctx % 4
    z = ((ctx // 4) % 2) * 4 + tp // 2
    core = tp % 2
    group = x // 2
    stays = core == group
    def device(at_x, at_y, at_z, at_core):
        at_z = at_z % 8
        return ((at_y % 4) * 8 + (at_z // 4) * 4 + at_x % 4, (at_z % 4) * 2 + at_core)

    beside_x = device(x + 1 - 2 * (x % 2), y, z, core)
    sibling = device(x, y, z, 1 - core)
    partner = device(x + 2, y, z, 1 - core)

    def beside_y(step):
        return device(x, y + step + 4, z, core)

    def on_line(l, dz):
        return device(x + 2 * l, y, z + dz, core)

    def copy_to(src, dst, send_sem, recv_sem, target):
        pltpu.make_async_remote_copy(
            src_ref=src, dst_ref=dst, send_sem=send_sem, recv_sem=recv_sem, device_id=target, device_id_type=MESH
        ).start()

    def take(ref, sem):
        pltpu.make_async_copy(ref, ref, sem).wait()

    barrier = pltpu.get_barrier_semaphore()
    greeted = [on_line(l, dz) for l, dz in LINES] + [beside_y(step) for step in (1, 2, 3)]
    greeted += [beside_x, sibling, partner]
    for target in greeted:
        pl.semaphore_signal(barrier, inc=1, device_id=target, device_id_type=MESH)
    k_load = pltpu.make_async_copy(k_in, k_ref, load.at[0])
    v_load = pltpu.make_async_copy(v_in, v_ref, load.at[1])
    k_load.start()
    v_load.start()

    @pl.when(stays)
    def _():
        pltpu.make_async_copy(q_in, q_ref, swap.at[1]).start()
        pltpu.make_async_copy(do_in, do_ref, swap.at[2]).start()

    totals[...] = jnp.zeros_like(totals)
    weighted[...] = jnp.zeros_like(weighted)
    dq_t[...] = jnp.zeros_like(dq_t)
    k_load.wait()
    v_load.wait()
    for h in range(HEADS):
        cols = slice(h * D, (h + 1) * D)
        k_unit[h], scale = unit(k_ref[:, cols].astype(F32))
        k_scale[h] = jnp.broadcast_to(scale, (16, D))
        mine[h, KEYS] = k_unit[h].astype(BF16)
        mine[h, VALUES] = v_ref[:, cols]
    pl.semaphore_wait(barrier, len(greeted))

    for l, dz in LINES:
        head = 2 * ((z + dz) % 4) + ((x + 2 * l) % 4) // 2
        spot = (l * 8 + (8 - dz) % 8) * 16
        copy_to(mine.at[head], kv.at[0, :, spot : spot + 16, :], z_sem.at[0], z_sem.at[1], on_line(l, dz))
    kv[0, :, 0:16, :] = mine[2 * (z % 4) + group]

    @pl.when(jnp.logical_not(stays))
    def _():
        copy_to(q_in, q_ref, swap.at[0], swap.at[1], partner)
        copy_to(do_in, do_ref, swap.at[3], swap.at[2], partner)

    others = kv.at[0, :, 16:BLOCK, :]
    take(others, z_sem.at[1])

    def along_x(kind, i, b, part_of=slice(0, BLOCK)):
        to = PLACE[1 - i, b]
        copy_to(kv.at[2 * PLACE[i, b], kind, part_of], kv.at[2 * to, kind, part_of], send, recv.at[kind, to], beside_x)

    def along_y(kind, i, b, part_of=slice(0, BLOCK)):
        for step in (1, 3, 2):
            to = PLACE[i, (b - step) % 4]
            copy_to(kv.at[2 * PLACE[i, b], kind, part_of], kv.at[2 * to, kind, part_of], send, recv.at[kind, to], beside_y(step))

    def got(kind, i, b):
        n = PLACE[i, b]
        take(kv.at[0, 0], recv.at[kind, n])
        if kind == KEYS and b == 0:
            along_y(kind, i, b)
        if kind == VALUES and i == 0:
            along_x(kind, i, b)
        copy_to(kv.at[2 * n, kind], kv.at[2 * n + 1, kind], s_send, s_recv.at[n], sibling)

    along_x(KEYS, 0, 0)
    along_y(VALUES, 0, 0)
    along_y(KEYS, 0, 0)
    along_x(VALUES, 0, 0)
    copy_to(kv.at[0], kv.at[1], s_send, s_recv.at[0], sibling)

    def pass_1(low, high):
        count = (high - low) * BLOCK
        scores = jnp.dot(kv[low:high, KEYS].reshape(count, D), q_t[...], preferred_element_type=F32)
        value_dots = jnp.dot(kv[low:high, VALUES].reshape(count, D), do_t[...], preferred_element_type=F32)
        e = jnp.exp2(scores * EXP2)
        raised[low:high] = e.reshape(high - low, BLOCK, ROWS)
        dots[low:high] = value_dots.reshape(high - low, BLOCK, ROWS)
        totals[...] += jnp.sum(e.reshape(count // 8, 8, ROWS), axis=0)
        weighted[...] += jnp.sum((e * value_dots).reshape(count // 8, 8, ROWS), axis=0)

    def run(body, low, high):
        body(low, high)

    def shared(i, b):
        take(kv.at[0], s_recv.at[PLACE[i, b]])

    take(q_ref, swap.at[1])
    for h in range(HEADS):
        cols = slice(h * D, (h + 1) * D)
        cast = unit(q_ref[:, cols].astype(F32))[0].astype(BF16)
        q_n[cols, :] = cast
        q_t[:, cols] = cast.T
    got(KEYS, 1, 0)
    for b in (3, 1, 2):
        got(VALUES, 0, b)
    take(do_ref, swap.at[2])
    for h in range(HEADS):
        cols = slice(h * D, (h + 1) * D)
        do_n[cols, :] = do_ref[:, cols]
        do_t[:, cols] = do_ref[:, cols].T
    def fetch(m):
        i, b = BLOCKS[m]
        if (i, b) != (1, 0):
            got(KEYS, i, b)
        if i:
            got(VALUES, i, b)

    run(pass_1, 0, 1)
    fetch(1)
    for m in range(1, 8):
        if m < 7:
            fetch(m + 1)
        shared(*BLOCKS[m - 1])
        run(pass_1, 2 * m - 1, 2 * m + 1)
    shared(*BLOCKS[7])
    run(pass_1, 15, 16)
    total = jnp.sum(totals[...], axis=0, keepdims=True)
    inverse = 1.0 / total
    rows[0:1, :] = inverse
    rows[1:2, :] = jnp.sum(weighted[...], axis=0, keepdims=True) * inverse

    def pass_2(low, high):
        count = (high - low) * BLOCK
        attend = raised[low:high].reshape(count, ROWS) * rows[0:1, :]
        score_grad = (attend * (dots[low:high].reshape(count, ROWS) - rows[1:2, :])).astype(BF16)
        value_part = jnp.dot(attend.astype(BF16), do_n[...], preferred_element_type=F32).astype(BF16)
        key_part = (jnp.dot(score_grad, q_n[...], preferred_element_type=F32) * INV).astype(BF16)
        part[low:high, VALUES] = value_part.reshape(high - low, BLOCK, D)
        part[low:high, KEYS] = key_part.reshape(high - low, BLOCK, D)
        grads[low:high] = score_grad.reshape(high - low, BLOCK, ROWS)

    def share(m):
        copy_to(part.at[2 * m + 1], sib_in.at[m], t_send, t_recv.at[m], sibling)

    def add(i, b, kind, *refs):
        n = 2 * PLACE[i, b]
        value = part[n, kind].astype(F32)
        for ref in refs:
            value = value + ref[...].astype(F32)
        part[n, kind] = value.astype(BF16)

    def settle(i, b):
        m = PLACE[i, b]
        take(kv.at[0], t_recv.at[m])
        came = [sib_in.at[m, VALUES]]
        if i == 0:
            take(kv.at[0, 0], xr_recv.at[b])
            came.append(x_in.at[b])
        add(i, b, VALUES, *came)
        if i == 1:
            copy_to(part.at[2 * m, VALUES], x_in.at[b], r_send, xr_recv.at[b], beside_x)
        elif b:
            copy_to(part.at[2 * m, VALUES], y_in.at[2, b - 1], r_send, yr_recv.at[2], beside_y(b))
        add(i, b, KEYS, sib_in.at[m, KEYS])
        if b:
            copy_to(part.at[2 * m, KEYS], y_in.at[i, b - 1], r_send, yr_recv.at[i], beside_y(b))

    def gather_y(which, i, kind, *more):
        take(y_in.at[0], yr_recv.at[which])
        add(i, 0, kind, y_in.at[which, 0], y_in.at[which, 1], y_in.at[which, 2], *more)

    run(pass_2, 15, 16)
    share(7)
    for m in range(6, -1, -1):
        run(pass_2, 2 * m + 1, 2 * m + 3)
        share(m)
        settle(*BLOCKS[m + 1])
        if BLOCKS[m + 1] == (0, 1):
            gather_y(1, 1, KEYS)
            copy_to(part.at[2 * PLACE[1, 0], KEYS], x_in.at[4], r_send, xr_recv.at[4], beside_x)
    run(pass_2, 0, 1)

    def query_part(n, carry):
        some = pl.ds(n * 4, 4)
        keys_t = kv[some, KEYS].reshape(4 * BLOCK, D).T
        dq_t[...] += jnp.dot(keys_t, grads[some].reshape(4 * BLOCK, ROWS), preferred_element_type=F32)
        return carry

    lax.fori_loop(0, 4, query_part, 0)
    for h in range(HEADS):
        cols = slice(h * D, (h + 1) * D)
        unit_rows, scale = unit(q_ref[:, cols].astype(F32))
        gq_out[:, cols] = unit_back(dq_t[:, cols].T * INV, unit_rows, scale).astype(BF16)

    @pl.when(jnp.logical_not(stays))
    def _():
        copy_to(gq_out, gq_in, back.at[0], back.at[1], partner)

    settle(0, 0)
    take(kv.at[0, 0], xr_recv.at[4])
    gather_y(0, 0, KEYS, x_in.at[4])
    gather_y(2, 0, VALUES)

    me = group * 8 + z
    for l, dz in LINES:
        spot = (l * 8 + dz) * 16
        copy_to(part.at[0, :, spot : spot + 16, :], line_in.at[me], l_sem.at[0], l_sem.at[1], on_line(l, dz))
    line_in[me] = part[0, :, 0:16, :]
    take(others, z_sem.at[0])
    take(kv.at[0:7], send)
    take(kv.at[0:8], s_send)
    take(part.at[0:8], t_send)
    take(part.at[0:7], r_send)

    @pl.when(stays)
    def _():
        gq_ref[...] = gq_out[...]

    @pl.when(jnp.logical_not(stays))
    def _():
        take(q_ref, swap.at[0])
        take(do_ref, swap.at[3])
        take(gq_out, back.at[0])
        take(gq_in, back.at[1])
        gq_ref[...] = gq_in[...]

    take(line_in.at[0 : LINE - 1], l_sem.at[1])
    for h in range(HEADS):
        cols = slice(h * D, (h + 1) * D)
        low = (h % 2) * 8 + h // 2
        sums = line_in[low].astype(F32) + line_in[low + 4].astype(F32)
        gk_ref[:, cols] = unit_back(sums[KEYS], k_unit[h], k_scale[h]).astype(BF16)
        gv_ref[:, cols] = sums[VALUES].astype(BF16)
    take(line_in.at[0 : LINE - 1], l_sem.at[0])


def hand_over(*refs):
    for source, target in zip(refs[:3], refs[3:]):
        target[...] = source[...]


def shards(query_raw, key_raw, values, grad_out):
    vmem = pl.BlockSpec(memory_space=pltpu.VMEM)
    anywhere = pl.BlockSpec(memory_space=pl.ANY)
    dma = pltpu.SemaphoreType.DMA
    outs = [jax.ShapeDtypeStruct(a.shape, BF16) for a in (query_raw, key_raw, values)]
    grads = pl.pallas_call(
        kernel,
        out_shape=[pltpu.VMEM(a.shape, a.dtype) for a in outs],
        in_specs=[anywhere] * 4,
        out_specs=[vmem] * 3,
        scratch_shapes=[
            pltpu.VMEM((D, ROWS), BF16),
            pltpu.VMEM((16, ROWS), BF16),
            pltpu.VMEM((16, ROWS), BF16),
            pltpu.VMEM((D, ROWS), BF16),
            pltpu.VMEM((D, ROWS), BF16),
            pltpu.VMEM((D, ROWS), BF16),
            pltpu.VMEM((ROWS, D), BF16),
            pltpu.VMEM((ROWS, D), BF16),
            pltpu.VMEM((16, BLOCK, ROWS), F32),
            pltpu.VMEM((16, BLOCK, ROWS), F32),
            pltpu.VMEM((16, BLOCK, ROWS), BF16),
            pltpu.VMEM((8, ROWS), F32),
            pltpu.VMEM((8, ROWS), F32),
            pltpu.VMEM((8, ROWS), F32),
            pltpu.VMEM((D, ROWS), F32),
            pltpu.VMEM((HEADS, 16, D), F32),
            pltpu.VMEM((HEADS, 16, D), F32),
            pltpu.VMEM((HEADS, 2, 16, D), BF16),
            pltpu.VMEM((16, 2, BLOCK, D), BF16),
            pltpu.VMEM((16, 2, BLOCK, D), BF16),
            pltpu.VMEM((8, 2, BLOCK, D), BF16),
            pltpu.VMEM((3, 3, BLOCK, D), BF16),
            pltpu.VMEM((5, BLOCK, D), BF16),
            pltpu.VMEM((LINE, 2, 16, D), BF16),
            pltpu.VMEM((D, ROWS), BF16),
            pltpu.VMEM((D, ROWS), BF16),
            dma((2,)),
            dma((4,)),
            dma((2,)),
            dma((2,)),
            dma,
            dma((2, 8)),
            dma,
            dma((8,)),
            dma,
            dma((8,)),
            dma,
            dma((3,)),
            dma((5,)),
            dma((2,)),
        ],
        compiler_params=pltpu.CompilerParams(
            collective_id=0, has_side_effects=True, vmem_limit_bytes=60 * 2**20
        ),
    )(query_raw, key_raw, values, grad_out)
    return pl.pallas_call(hand_over, out_shape=outs, in_specs=[vmem] * 3, out_specs=[vmem] * 3)(
        *[pltpu.with_memory_space_constraint(grad, pltpu.VMEM) for grad in grads]
    )


def solution(mesh):
    split = (P("ctx", "tp"), P(("ctx", "tp"), None), P(("ctx", "tp"), None), P("ctx", "tp"))
    return jax.shard_map(
        shards, mesh=mesh, in_specs=split, out_specs=split[:3], check_vma=False
    )
```
